256 devices in a mesh: row: 32 (over x, y, core), col: 8 (over z).
Axes of the slice: x: 4, y: 4, z: 8, core: 2. Of those that a mesh axis runs over, the one named last changes fastest.
Arguments:
- solution: float32 [64, 65536], P(None, ('row', 'col')), may hold values from -6 to 6
- residual: float32 [64, 262144], P(None, ('row', 'col')), may hold values from -6 to 6
- direction: float32 [64, 65536], P(None, ('row', 'col')), may hold values from -6 to 6
- jacobian_tiles: bfloat16 [2048, 40, 128, 128], P('row', 'col'), may hold values from -0.078125 to 0.078125
- tile_blocks: int32 [2048, 40], P('row', 'col'), may hold values from 0 to 63, as said below
- tile_counts: int32 [2048, 8], P('row', 'col'), may hold values from 1 to 5, as said below
Outputs:
- solution_next: float32 [64, 65536], P(None, ('row', 'col'))
- residual_next: float32 [64, 262144], P(None, ('row', 'col'))
- direction_next: float32 [64, 65536], P(None, ('row', 'col'))
The draws below stay inside these ranges and needn't reach their ends.
Inputs may be any that keep to these rules, and one draw needn't show every extreme that they name: `tile_blocks`: within each sensor and parameter group the 5 entries are different. Only the first tile_counts[i, c] slots of sensor i in group c hold a tile; some sensor fills all 5 slots of every group.
All inputs are finite; a program needn't handle non-finite values.
Results may differ from the reference program's by a relative error of at most 0.023.
Values may be sent and summed in bfloat16 or wider, within the bound.
A program may use at most 128 MiB of HBM per device.

```python
import jax
import jax.numpy as jnp
from jax import lax

TB = 128
NRHS = 64
CB_DEV = 64
SLOT = 5
ITERS = 2
RB_DEV = 64
NRB = 2048
NROWS = 262144
NPB = 512
NPAR = 65536
SHARD_BLOCKS = 2
N_ROW = 32
N_COL = 8


def draw_tile_blocks(key, part):
    groups = NPB // CB_DEV
    base = jax.random.fold_in(key, 3)
    subkeys = jax.random.split(base, NRB * groups)

    def choose_blocks(subkey):
        return jax.random.permutation(subkey, CB_DEV)[:SLOT]
    picks = jax.vmap(choose_blocks)(subkeys)
    return picks.reshape(NRB, groups * SLOT).astype(jnp.int32)


def draw_tile_counts(key, part):
    groups = NPB // CB_DEV
    base = jax.random.fold_in(key, 5)
    values = jax.random.randint(base, (NRB, groups), 1, SLOT + 1)
    chosen = jax.random.randint(jax.random.fold_in(base, 11), (), 0, NRB)
    marker = (jnp.arange(NRB) == chosen)[:, None]
    return jnp.where(marker, SLOT, values).astype(jnp.int32)


def levels(key, dims, shards, smallest, largest):
    def one(dim, shards_of):
        draws = jax.random.uniform(jax.random.fold_in(jax.random.fold_in(key, 6), dim), (shards_of,), jnp.float32, smallest / len(shards), largest / len(shards))
        return jnp.repeat(jnp.exp(draws), dims[dim] // shards_of).reshape((-1,) + (1,) * (len(dims) - dim - 1))

    loudness = one(*shards[0])
    for cut in shards[1:]:
        loudness = loudness * one(*cut)
    return loudness


def normal_values(rng, extent, width, limit, cuts=(), kind=jnp.bfloat16):
    level = levels(rng, extent, cuts, -0.22, 0.18) if cuts else 1.0
    array = jax.random.normal(rng, extent, jnp.float32) * width * level
    return jnp.minimum(jnp.maximum(array, -limit), limit).astype(kind)


def setup_inputs(seed: int = 0) -> dict:
    seeds = jax.random.split(jax.random.key(seed), 7)
    solution = normal_values(seeds[0], (NRHS, NPAR), 1.0, 6.0, ((1, 256),), jnp.float32)
    residual = normal_values(seeds[1], (NRHS, NROWS), 1.0, 6.0, ((1, 256),), jnp.float32)
    direction = normal_values(seeds[2], (NRHS, NPAR), 1.0, 6.0, ((1, 256),), jnp.float32)
    jacobian_tiles = normal_values(seeds[3], (NRB, N_COL * SLOT, TB, TB), (TB * SLOT * N_COL) ** -0.5, 0.078125, ((0, 32), (1, 8)))
    tile_blocks = draw_tile_blocks(jax.random.fold_in(seeds[6], 71), 0)
    tile_counts = draw_tile_counts(jax.random.fold_in(seeds[6], 71), 0)
    return {"solution": solution, "residual": residual, "direction": direction, "jacobian_tiles": jacobian_tiles, "tile_blocks": tile_blocks, "tile_counts": tile_counts}


def times_highest(left, right):
    return jnp.dot(left, right, precision=lax.Precision.HIGHEST)

def gram_matrix(values):
    return jnp.dot(values, values.T, precision=lax.Precision.HIGHEST)

def solve_spd(matrix, right):
    factor_low = jnp.linalg.cholesky(matrix)
    middle = lax.linalg.triangular_solve(factor_low, right, left_side=True, lower=True)
    return lax.linalg.triangular_solve(factor_low, middle, left_side=True, lower=True, transpose_a=True)

def block_index(tile_blocks):
    groups = NPB // CB_DEV
    slots = jnp.arange(groups * SLOT, dtype=jnp.int32)
    group_of = (slots // SLOT)[None, :]
    owner = tile_blocks // SHARD_BLOCKS
    within = tile_blocks % SHARD_BLOCKS
    return ((owner * groups + group_of) * SHARD_BLOCKS + within).astype(jnp.int32)

def live_mask(tile_counts):
    slots = jnp.arange(NPB // CB_DEV * SLOT, dtype=jnp.int32)
    limits = jnp.repeat(tile_counts, SLOT, axis=1)
    return (slots[None, :] % SLOT < limits).astype(jnp.float32)

def forward(jacobian_tiles, blocks, live_slot, direction_half):
    groups = NPB // CB_DEV
    table_view = direction_half.reshape(NRHS, NPB, TB)
    tile_sets = jacobian_tiles.reshape(N_ROW, RB_DEV, groups * SLOT, TB, TB)
    block_sets = blocks.reshape(N_ROW, RB_DEV, groups * SLOT)
    live_sets = live_slot.reshape(N_ROW, RB_DEV, groups * SLOT)

    def one_range(pieces):
        tile_blk, index_blk, live_blk = pieces
        picked = jnp.take(table_view, index_blk, axis=1).astype(jnp.float32) * live_blk[None, :, :, None]
        product = jnp.einsum('rjab,nrjb->nrja', tile_blk.astype(jnp.float32), picked)
        product = product.reshape(NRHS, RB_DEV, groups, SLOT, TB).sum(axis=3)
        rounded = product.astype(jnp.bfloat16).astype(jnp.float32)
        return rounded.sum(axis=2).reshape(NRHS, RB_DEV * TB)
    ranges = lax.map(one_range, (tile_sets, block_sets, live_sets))
    return ranges.transpose(1, 0, 2).reshape(NRHS, NROWS)

def backward(jacobian_tiles, blocks, live_slot, rows_half):
    groups = NPB // CB_DEV
    row_sets = rows_half.reshape(NRHS, N_ROW, RB_DEV, TB).transpose(1, 0, 2, 3)
    tile_sets = jacobian_tiles.reshape(N_ROW, RB_DEV, groups * SLOT, TB, TB)
    block_sets = blocks.reshape(N_ROW, RB_DEV, groups * SLOT)
    live_sets = live_slot.reshape(N_ROW, RB_DEV, groups * SLOT)

    def one_range(running, pieces):
        tile_blk, index_blk, live_blk, row_blk = pieces
        contrib = jnp.einsum('rjab,nra->rjnb', tile_blk.astype(jnp.float32), row_blk.astype(jnp.float32))
        contrib = contrib * live_blk[:, :, None, None]
        added = jax.ops.segment_sum(contrib.reshape(-1, NRHS, TB), index_blk.reshape(-1), num_segments=NPB)
        return (running + added, None)
    start = jnp.zeros((NPB, NRHS, TB), jnp.float32)
    running, _ = lax.scan(one_range, start, (tile_sets, block_sets, live_sets, row_sets))
    return running.transpose(1, 0, 2).reshape(NRHS, NPAR)

def reference(solution, residual, direction, jacobian_tiles, tile_blocks, tile_counts):
    blocks = block_index(tile_blocks)
    live_slot = live_mask(tile_counts)
    gradient = backward(jacobian_tiles, blocks, live_slot, residual.astype(jnp.bfloat16))
    gamma_now = gram_matrix(gradient)
    for iteration in range(ITERS):
        image = forward(jacobian_tiles, blocks, live_slot, direction.astype(jnp.bfloat16))
        curvature = gram_matrix(image)
        step_alpha = solve_spd(curvature, gamma_now)
        solution = solution + times_highest(step_alpha.T, direction)
        residual = residual - times_highest(step_alpha.T, image)
        gradient = backward(jacobian_tiles, blocks, live_slot, residual.astype(jnp.bfloat16))
        gamma_next = gram_matrix(gradient)
        step_beta = solve_spd(gamma_now, gamma_next)
        direction = gradient + times_highest(step_beta.T, direction)
        gamma_now = gamma_next
    return (solution, residual, direction)
```

```python
import functools

import jax
import jax.numpy as jnp
from jax import lax
from jax.experimental import pallas as pl
from jax.experimental.pallas import tpu as pltpu
from jax.sharding import PartitionSpec as P

MESH = pl.DeviceIdType.MESH
F32, BF16 = jnp.float32, jnp.bfloat16
TB = 128
HOPS = 4
HIGH = lax.Precision.HIGHEST


def dot_high(left, right):
    return jnp.dot(left, right, precision=HIGH, preferred_element_type=F32)


def dot_lanes(left, right, precision=None):
    return lax.dot_general(
        left, right, (((1,), (1,)), ((), ())), precision=precision, preferred_element_type=F32
    )


def gram(value):
    return dot_lanes(value, value, HIGH)


def side_by_side(parts):
    return jnp.concatenate(parts, axis=1)


def inverses(matrices):
    size = matrices[0].shape[0]
    rows = lax.broadcasted_iota(jnp.int32, (size, 2 * size), 0)
    lanes = lax.broadcasted_iota(jnp.int32, (size, 2 * size), 1)
    eye = jnp.where(rows + size == lanes, 1.0, 0.0).astype(F32)[:, size:]

    def step(k, works):
        done = []
        for work in works:
            row = jnp.sum(jnp.where(rows == k, work, 0.0), axis=0, keepdims=True)
            col = jnp.sum(jnp.where(lanes == k, work, 0.0), axis=1, keepdims=True)
            pivot = jnp.sum(jnp.where(lanes[:1] == k, row, 0.0), axis=1, keepdims=True)
            row = row / pivot
            done.append(jnp.where(rows == k, row, work - col * row))
        return tuple(done)

    works = lax.fori_loop(0, size, step, tuple(side_by_side([a, eye]) for a in matrices))
    return [work[:, size:] for work in works]


class Ring:
    @staticmethod
    def exists(d, t, h):
        return 1 <= t <= HOPS and (t < HOPS or h == d)


def kernel(
    ny,
    slots,
    gidx,
    perm,
    keep,
    last,
    has,
    sol_ref,
    res_ref,
    dir_ref,
    tiles_hbm,
    sol_out,
    res_out,
    dir_out,
    tiles,
    contrib,
    prefix,
    dirbuf,
    gbuf,
    rowsbuf,
    imgbuf,
    part,
    ringout,
    ringland,
    imgshare,
    xout,
    xland,
    sbuf,
    rland,
    gshare,
    hshare,
    dnext,
    ar_in,
    ar_z,
    ar_c,
    ar_x,
    ar_out,
    tile_sem,
    ring_send,
    ring_recv,
    agr_send,
    agr_recv,
    fwd_send,
    fwd_recv,
    x_send,
    x_recv,
    rs_send,
    rs_recv,
    ar_send,
    ar_recv,
):
    rows, cols = lax.axis_size("row"), lax.axis_size("col")
    chips = rows // 2
    nx = chips // ny
    r, z = lax.axis_index("row"), lax.axis_index("col")
    core, chip = lax.rem(r, 2), r // 2
    cx, cy = chip // ny, lax.rem(chip, ny)
    share = res_ref.shape[1] // TB
    half = share // 2
    blocks = 2 * rows
    hb = blocks // 2
    group = 2 * ny
    rhs = res_ref.shape[0]

    def at_col(d):
        return lax.rem(z + d + cols, cols)

    def ring_dev(d):
        return (r, at_col(1 if d == 0 else -1))

    sibling = (r + 1 - 2 * core, z)

    def chip_at(dx, dy):
        return lax.rem(cx + dx, nx) * ny + lax.rem(cy + dy, ny)

    offsets = [(dx, dy) for dx in range(nx) for dy in range(ny)]
    others = sorted(
        offsets[1:], key=lambda o: (-(min(o[0], nx - o[0]) + min(o[1], ny - o[1])), o)
    )

    def remote(src, dst, ss, rs, dev):
        return pltpu.make_async_remote_copy(
            src_ref=src, dst_ref=dst, send_sem=ss, recv_sem=rs, device_id=dev, device_id_type=MESH
        )

    per_chunk = share * slots
    chunk_copies = []
    for c in range(cols):
        cc = at_col(cols // 2 + c) if False else c
        chunk_copies.append(
            pltpu.make_async_copy(
                tiles_hbm.at[pl.ds(cc * per_chunk, per_chunk)],
                tiles.at[pl.ds(cc * per_chunk, per_chunk)],
                tile_sem.at[c],
            )
        )
        chunk_copies[-1].start()

    mine = core * hb + 2 * chip
    for j in range(2):
        dirbuf[mine + j] = dir_ref[:, j * TB : (j + 1) * TB].astype(BF16)
    dirbuf[blocks] = jnp.zeros((rhs, TB), BF16)
    gbuf[blocks] = jnp.zeros((rhs, TB), BF16)
    for i in range(share):
        rowsbuf[z * share + i] = res_ref[:, i * TB : (i + 1) * TB].astype(BF16)

    barrier = pltpu.get_barrier_semaphore()
    partners = [sibling]
    partners += [(chip_at(*o) * 2 + core, z) for o in others]
    partners += [(r, at_col(d)) for d in range(1, cols)]
    for dev in partners:
        pl.semaphore_signal(barrier, inc=1, device_id=dev, device_id_type=MESH)
    pl.semaphore_wait(barrier, len(partners))

    def sensor_tiles(sensor):
        return side_by_side([tiles[sensor * slots + s] for s in range(slots)])

    def grad_piece(buf, shard, h):
        def one(i, _):
            sensor = shard * share + h * half + i
            value = jnp.dot(buf[sensor], sensor_tiles(sensor), preferred_element_type=F32)
            for s in range(slots):
                contrib[sensor * slots + s] = value[:, s * TB : (s + 1) * TB]
            return 0

        lax.fori_loop(0, half, one, 0, unroll=True)

    def image_piece(buf, dest, h):
        def one(i, _):
            sensor = dest * share + h * half + i
            picked = side_by_side([buf[gidx[sensor * slots + s]] for s in range(slots)])
            part[i] = dot_lanes(picked, sensor_tiles(sensor))
            return 0

        lax.fori_loop(0, half, one, 0, unroll=True)

    def sorted_sums():
        def one(j, run):
            run = run * keep[j] + contrib[perm[j]]
            prefix[j] = run
            return run

        lax.fori_loop(0, contrib.shape[0], one, jnp.zeros((rhs, TB), F32), unroll=4)

    def block_sum(k):
        return prefix[last[k]] * has[k]

    def ring_gather(buf, ss, rs):
        def piece(d, t, h):
            step = (t - 1) if d == 0 else (1 - t)
            return buf.at[pl.ds(at_col(-step) * share + h * half, half)]

        def hop(d, t, h):
            ref = piece(d, t, h)
            return remote(ref, ref, ss.at[d, t - 1, h], rs.at[d, t - 1, h], ring_dev(d))

        def landed(d, t, h):
            ref = piece(d, t + 1, h)
            return remote(ref, ref, ss.at[d, t - 1, h], rs.at[d, t - 1, h], ring_dev(d))

        for h in range(2):
            for d in range(2):
                hop(d, 1, h).start()
        for h in range(2):
            yield (z, h)
        for t in range(1, HOPS + 1):
            for h in range(2):
                for d in range(2):
                    if not Ring.exists(d, t, h):
                        continue
                    landed(d, t, h).wait_recv()
                    if Ring.exists(d, t + 1, h):
                        hop(d, t + 1, h).start()
                    yield (at_col(-t if d == 0 else t), h)
        for t in range(1, HOPS + 1):
            for h in range(2):
                for d in range(2):
                    if Ring.exists(d, t, h):
                        hop(d, t, h).wait_send()

    def ring_scatter(buf, land, out, ss, rs, wait_tiles):
        def hop(d, t, h):
            return remote(
                ringout.at[d, t - 1, h],
                land.at[d, t - 1, h],
                ss.at[d, t - 1, h],
                rs.at[d, t - 1, h],
                ring_dev(d),
            )

        def came(d, t, h):
            return Ring.exists(d, HOPS + 1 - t, h)

        order = []
        for t in range(1, HOPS + 1):
            for h in range(2):
                for d in range(2):
                    if came(d, t, h):
                        order.append((0 if not (t > 1 and came(d, t - 1, h)) else t, t, h, d))
        for _, t, h, d in sorted(order):
            away = HOPS + 1 - t
            dest = at_col(away if d == 0 else -away)
            image_piece(buf, dest, h)
            if t > 1 and came(d, t - 1, h):
                hop(d, t - 1, h).wait_recv()
                for i in range(half):
                    ringout[d, t - 1, h, i] = (part[i] + land[d, t - 2, h, i].astype(F32)).astype(BF16)
            else:
                for i in range(half):
                    ringout[d, t - 1, h, i] = part[i].astype(BF16)
            hop(d, t, h).start()
            yield
        for h in range(2):
            image_piece(buf, z, h)
            for d in range(2):
                hop(d, HOPS, h).wait_recv()
            for i in range(half):
                total = part[i]
                for d in range(2):
                    total = total + land[d, HOPS - 1, h, i].astype(F32)
                out[h * half + i] = total
            yield
        for t in range(1, HOPS + 1):
            for h in range(2):
                for d in range(2):
                    if came(d, t, h):
                        hop(d, t, h).wait_send()

    def plane(dx):
        return lax.rem(cx + dx, nx)

    def row_gather(buf, n):
        own = buf.at[pl.ds(mine, 2)]
        for dx, dy in others:
            remote(
                own,
                own,
                agr_send.at[n],
                agr_recv.at[n, (nx - dx) % nx],
                (chip_at(dx, dy) * 2 + core, z),
            ).start()

        def forward(dx, side):
            ref = buf.at[pl.ds(side * hb + plane(dx) * group, group)]
            return remote(ref, ref, fwd_send.at[n, dx], fwd_recv.at[n, dx], sibling)

        order = sorted(range(nx), key=lambda dx: min(dx, nx - dx))
        yield
        for dx in order:
            count = group if dx else group - 2
            ref = buf.at[pl.ds(core * hb, count)]
            if count:
                remote(ref, ref, agr_send.at[n], agr_recv.at[n, dx], sibling).wait_recv()
            forward(dx, core).start()
            yield
        for dx in order:
            forward(dx, 1 - core).wait_recv()
        yield
        for dx in order:
            forward(dx, core).wait_send()
        ref = buf.at[pl.ds(0, 2 * len(others))]
        remote(ref, ref, agr_send.at[n], agr_recv.at[n, 0], sibling).wait_send()

    def row_scatter(n, out):
        def swap(u):
            return remote(
                xout.at[pl.ds(u * group, group)],
                xland.at[n, pl.ds(u * group, group)],
                x_send.at[n, u],
                x_recv.at[n, u],
                sibling,
            )

        for u in range(nx):
            base = (1 - core) * hb + u * group
            for b in range(group):
                xout[u * group + b] = block_sum(base + b).astype(BF16)
            swap(u).start()
        yield
        slot = {o: i for i, o in enumerate(offsets[1:])}
        for u in range(nx):
            swap(u).wait_recv()
            base = core * hb + u * group
            for b in range(group):
                total = block_sum(base + b) + xland[n, u * group + b].astype(F32)
                sbuf[u * group + b] = total.astype(BF16)
            yield
        for o in others:
            remote(
                sbuf.at[pl.ds(2 * chip_at(*o), 2)],
                rland.at[n, pl.ds(2 * slot[o], 2)],
                rs_send.at[n],
                rs_recv.at[n],
                (chip_at(*o) * 2 + core, z),
            ).start()
        for j in range(2):
            out[j] = block_sum(mine + j) + xland[n, 2 * chip + j].astype(F32)
        yield
        every = rland.at[n]
        remote(every, every, rs_send.at[n], rs_recv.at[n], sibling).wait_recv()
        for j in range(2):
            total = out[j]
            for i in range(len(others)):
                total = total + rland[n, 2 * i + j].astype(F32)
            out[j] = total
        yield
        remote(every, every, rs_send.at[n], rs_recv.at[n], sibling).wait_send()
        for u in range(nx):
            swap(u).wait_send()

    strip = rhs // cols

    def all_sum(n, value):
        ar_in[n] = value
        for d in range(1, cols):
            peer = at_col(d)
            remote(
                ar_in.at[n, pl.ds(peer * strip, strip)],
                ar_z.at[n, pl.ds((d - 1) * strip, strip)],
                ar_send.at[n, 0],
                ar_recv.at[n, 0],
                (r, peer),
            ).start()
        yield
        ref = ar_z.at[n]
        remote(ref, ref, ar_send.at[n, 0], ar_recv.at[n, 0], sibling).wait_recv()
        total = ar_in[n, pl.ds(z * strip, strip)]
        for d in range(1, cols):
            total = total + ar_z[n, (d - 1) * strip : d * strip]
        ar_c[n, 0] = total
        swap = remote(ar_c.at[n, 0], ar_c.at[n, 1], ar_send.at[n, 1], ar_recv.at[n, 1], sibling)
        swap.start()
        yield
        swap.wait_recv()
        total = total + ar_c[n, 1]
        ar_x[n, chip] = total
        own = ar_x.at[n, chip]
        for o in others:
            remote(
                own, own, ar_send.at[n, 2], ar_recv.at[n, 2], (chip_at(*o) * 2 + core, z)
            ).start()
        yield
        ref = ar_x.at[n, pl.ds(0, len(others))]
        remote(ref, ref, ar_send.at[n, 2], ar_recv.at[n, 2], sibling).wait_recv()
        total = ar_x[n, 0]
        for i in range(1, chips):
            total = total + ar_x[n, i]
        mine_rows = ar_out.at[n, pl.ds(z * strip, strip)]
        ar_out[n, pl.ds(z * strip, strip)] = total
        for d in range(1, cols):
            remote(
                mine_rows, mine_rows, ar_send.at[n, 3], ar_recv.at[n, 3], (r, at_col(d))
            ).start()
        yield
        ref = ar_out.at[n, pl.ds(0, (cols - 1) * strip)]
        remote(ref, ref, ar_send.at[n, 3], ar_recv.at[n, 3], sibling).wait_recv()
        yield
        for s, whole in ((0, ar_z.at[n]), (2, ar_x.at[n, pl.ds(0, len(others))]), (3, ref)):
            remote(whole, whole, ar_send.at[n, s], ar_recv.at[n, s], sibling).wait_send()
        swap.wait_send()

    def advance(gen, times=1):
        for _ in range(times):
            next(gen, None)

    def finish(gen):
        for _ in gen:
            pass

    def wide(ref):
        return side_by_side([ref[i] for i in range(ref.shape[0])])

    def to_blocks(value):
        return [value[:, i * TB : (i + 1) * TB] for i in range(value.shape[1] // TB)]

    def pair(left, right):
        return side_by_side([left, right])

    resid = ring_gather(rowsbuf, ring_send.at[0], ring_recv.at[0])
    first = next(resid)
    direct = row_gather(dirbuf, 0)
    advance(direct)
    for c in chunk_copies:
        c.wait()

    def grad_next(gen, buf, times):
        for _ in range(times):
            got = next(gen, None)
            if got is not None:
                grad_piece(buf, *got)

    grad_piece(rowsbuf, *first)
    grad_next(resid, rowsbuf, 3)
    advance(direct, 2)
    grad_next(resid, rowsbuf, 2)
    advance(direct, nx - 1)
    scat = ring_scatter(dirbuf, ringland.at[0], imgshare.at[0], ring_send.at[1], ring_recv.at[1], None)
    for _ in range(8):
        advance(scat)
        grad_next(resid, rowsbuf, 2)
    finish(resid)
    sorted_sums()
    rowsc = row_scatter(0, gshare)
    advance(rowsc)
    advance(scat, 3)
    advance(rowsc, nx + 1)
    finish(scat)
    finish(direct)

    inv_prev = None
    for it in range(2):
        if it == 1:
            add = to_blocks(dot_high(beta_t, wide(imgshare.at[0])))
            for i in range(share):
                imgshare[1, i] = imgshare[1, i] + add[i]
        for i in range(share):
            imgbuf[it, z * share + i] = imgshare[it, i].astype(BF16)
        gather = ring_gather(imgbuf.at[it], ring_send.at[2 + 2 * it], ring_recv.at[2 + 2 * it])
        first = next(gather)
        if it == 0:
            finish(rowsc)
            gamma_part = gram(wide(gshare))
        else:
            gamma_part = jnp.zeros((rhs, rhs), F32)
        summed = all_sum(it, pair(gram(wide(imgshare.at[it])), gamma_part))
        advance(summed)
        grad_piece(imgbuf.at[it], *first)
        grad_next(gather, imgbuf.at[it], 3)
        advance(summed)
        grad_next(gather, imgbuf.at[it], 2)
        advance(summed)
        grad_next(gather, imgbuf.at[it], 2)
        advance(summed)
        grad_next(gather, imgbuf.at[it], 4)
        advance(summed)
        grad_next(gather, imgbuf.at[it], 4)
        finish(summed)
        finish(gather)
        both = ar_out[it]
        curvature = both[:, :rhs]
        if it == 0:
            gamma = both[:, rhs:]
        sorted_sums()
        rowsc = row_scatter(1 + it, hshare)
        advance(rowsc, nx + 2)
        inv_curv, inv_gamma = inverses([curvature, gamma])
        alpha_t = dot_high(gamma, inv_curv)
        finish(rowsc)
        step_g = to_blocks(dot_high(alpha_t, wide(hshare)))
        for j in range(2):
            gshare[j] = gshare[j] - step_g[j]
            if it == 0:
                gbuf[mine + j] = gshare[j].astype(BF16)
        if it == 0:
            direct = row_gather(gbuf, 1)
            advance(direct)
        new_gamma = gram(wide(gshare))
        summed = all_sum(2 + it, pair(new_gamma, jnp.zeros((rhs, rhs), F32)))
        advance(summed)
        old_dir = dir_ref[...] if it == 0 else wide(dnext)
        old_sol = sol_ref[...] if it == 0 else sol_out[...]
        old_res = res_ref[...] if it == 0 else res_out[...]
        sol_out[...] = old_sol + dot_high(alpha_t, old_dir)
        res_out[...] = old_res - dot_high(alpha_t, wide(imgshare.at[it]))
        if it == 0:
            advance(summed)
            advance(direct, nx + 1)
            advance(summed)
            scat = ring_scatter(
                gbuf, ringland.at[1], imgshare.at[1], ring_send.at[3], ring_recv.at[3], None
            )
            advance(scat, 4)
            advance(summed)
            advance(scat, 4)
            finish(summed)
        else:
            finish(summed)
        gamma_next = ar_out[2 + it][:, :rhs]
        beta_t = dot_high(gamma_next, inv_gamma)
        step_d = dot_high(beta_t, old_dir)
        if it == 0:
            for j, value in enumerate(to_blocks(step_d)):
                dnext[j] = gshare[j] + value
            finish(scat)
            finish(direct)
        else:
            dir_out[...] = wide(gshare) + step_d
        gamma = gamma_next


def index_tables(tile_blocks, tile_counts, blocks):
    sensors, slots = tile_blocks.shape
    live = jnp.arange(slots, dtype=jnp.int32)[None, :] < tile_counts
    k = tile_blocks
    place = (k // 4) * 2 + k % 2 + ((k // 2) % 2) * (blocks // 2)
    gidx = jnp.where(live, place, blocks).reshape(-1)
    entries = sensors * slots
    order = jnp.arange(entries, dtype=jnp.int32)
    key = gidx * entries + order
    rank = jnp.sum((key[None, :] < key[:, None]).astype(jnp.int32), axis=1)
    at = rank[None, :] == order[:, None]
    perm = jnp.sum(jnp.where(at, order[None, :], 0), axis=1)
    block_of = jnp.sum(jnp.where(at, gidx[None, :], 0), axis=1)
    same = jnp.concatenate([jnp.zeros((1,), bool), block_of[1:] == block_of[:-1]])
    every = jnp.arange(blocks, dtype=jnp.int32)
    upto = jnp.sum((gidx[None, :] <= every[:, None]).astype(jnp.int32), axis=1)
    has = jnp.any(gidx[None, :] == every[:, None], axis=1)
    return (gidx, perm, same.astype(F32), jnp.maximum(upto - 1, 0), has.astype(F32))


def per_device(solution, residual, direction, jacobian_tiles, tile_blocks, tile_counts):
    rows, cols = lax.axis_size("row"), lax.axis_size("col")
    chips = rows // 2
    ny = 4 if chips % 4 == 0 else chips
    nx = chips // ny
    rhs = residual.shape[0]
    sensors, slots = tile_blocks.shape
    entries = sensors * slots
    blocks = 2 * rows
    share = residual.shape[1] // TB
    half = share // 2
    tables = index_tables(tile_blocks, tile_counts, blocks)
    tile = (rhs, TB)
    strip = rhs // cols
    vmem = pl.BlockSpec(memory_space=pltpu.VMEM)
    smem = pl.BlockSpec(memory_space=pltpu.SMEM)
    dma = pltpu.SemaphoreType.DMA
    return pl.pallas_call(
        functools.partial(kernel, ny, slots),
        out_shape=[
            jax.ShapeDtypeStruct(solution.shape, F32),
            jax.ShapeDtypeStruct(residual.shape, F32),
            jax.ShapeDtypeStruct(direction.shape, F32),
        ],
        in_specs=[smem] * 5 + [vmem] * 3 + [pl.BlockSpec(memory_space=pl.ANY)],
        out_specs=[vmem] * 3,
        scratch_shapes=[
            pltpu.VMEM((entries, TB, TB), BF16),
            pltpu.VMEM((entries, *tile), F32),
            pltpu.VMEM((entries, *tile), F32),
            pltpu.VMEM((blocks + 1, *tile), BF16),
            pltpu.VMEM((blocks + 1, *tile), BF16),
            pltpu.VMEM((sensors, *tile), BF16),
            pltpu.VMEM((2, sensors, *tile), BF16),
            pltpu.VMEM((half, *tile), F32),
            pltpu.VMEM((2, HOPS, 2, half, *tile), BF16),
            pltpu.VMEM((2, 2, HOPS, 2, half, *tile), BF16),
            pltpu.VMEM((2, share, *tile), F32),
            pltpu.VMEM((blocks // 2, *tile), BF16),
            pltpu.VMEM((3, blocks // 2, *tile), BF16),
            pltpu.VMEM((blocks // 2, *tile), BF16),
            pltpu.VMEM((3, 2 * (chips - 1), *tile), BF16),
            pltpu.VMEM((2, *tile), F32),
            pltpu.VMEM((2, *tile), F32),
            pltpu.VMEM((2, *tile), F32),
            pltpu.VMEM((4, rhs, TB), F32),
            pltpu.VMEM((4, (cols - 1) * strip, TB), F32),
            pltpu.VMEM((4, 2, strip, TB), F32),
            pltpu.VMEM((4, chips, strip, TB), F32),
            pltpu.VMEM((4, rhs, TB), F32),
            dma((cols,)),
            dma((5, 2, HOPS, 2)),
            dma((5, 2, HOPS, 2)),
            dma((2,)),
            dma((2, nx)),
            dma((2, nx)),
            dma((2, nx)),
            dma((3, nx)),
            dma((3, nx)),
            dma((3,)),
            dma((3,)),
            dma((4, 4)),
            dma((4, 4)),
        ],
        compiler_params=pltpu.CompilerParams(
            collective_id=0, has_side_effects=True, vmem_limit_bytes=58 * 1024 * 1024
        ),
    )(*tables, solution, residual, direction, jacobian_tiles.reshape(entries, TB, TB))


def solution(mesh):
    both = P(None, ("row", "col"))
    return jax.shard_map(
        per_device,
        mesh=mesh,
        in_specs=(both, both, both, P("row", "col", None, None), P("row", "col"), P("row", "col")),
        out_specs=(both, both, both),
        check_vma=False,
    )
```

```python
import functools

import jax
import jax.numpy as jnp
from jax import lax
from jax.experimental import pallas as pl
from jax.experimental.pallas import tpu as pltpu
from jax.sharding import PartitionSpec as P

MESH = pl.DeviceIdType.MESH
F32, BF16 = jnp.float32, jnp.bfloat16
TB = 128
HOPS = 4
PIECES = 4
HIGH = lax.Precision.HIGHEST


def dot_high(left, right):
    return jnp.dot(left, right, precision=HIGH, preferred_element_type=F32)


def dot_lanes(left, right, precision=None):
    return lax.dot_general(
        left, right, (((1,), (1,)), ((), ())), precision=precision, preferred_element_type=F32
    )


def gram(value):
    return dot_lanes(value, value, HIGH)


def side_by_side(parts):
    return jnp.concatenate(parts, axis=1)


def inverses(matrices):
    size = matrices[0].shape[0]
    rows = lax.broadcasted_iota(jnp.int32, (size, 2 * size), 0)
    lanes = lax.broadcasted_iota(jnp.int32, (size, 2 * size), 1)
    eye = jnp.where(rows + size == lanes, 1.0, 0.0).astype(F32)[:, size:]

    def step(k, works):
        done = []
        for work in works:
            row = jnp.sum(jnp.where(rows == k, work, 0.0), axis=0, keepdims=True)
            col = jnp.sum(jnp.where(lanes == k, work, 0.0), axis=1, keepdims=True)
            pivot = jnp.sum(jnp.where(lanes[:1] == k, row, 0.0), axis=1, keepdims=True)
            row = row / pivot
            done.append(jnp.where(rows == k, row, work - col * row))
        return tuple(done)

    works = lax.fori_loop(0, size, step, tuple(side_by_side([a, eye]) for a in matrices))
    return [work[:, size:] for work in works]


def kernel(
    ny,
    slots,
    blocks_ref,
    counts_ref,
    sol_ref,
    res_ref,
    dir_ref,
    tiles_hbm,
    sol_out,
    res_out,
    dir_out,
    tiles,
    contrib,
    prefix,
    dirbuf,
    gbuf,
    rowsbuf,
    imgbuf,
    part,
    ringout,
    ringland,
    imgshare,
    xout,
    xland,
    sbuf,
    rland,
    gshare,
    hshare,
    dnext,
    ar_in,
    ar_sib,
    ar_x,
    ar_z,
    ar_out,
    keys_v,
    keys_s,
    table_v,
    table_s,
    table_sem,
    tile_sem,
    ring_send,
    ring_recv,
    agr_send,
    agr_recv,
    fwd_send,
    fwd_recv,
    x_send,
    x_recv,
    rs_send,
    rs_recv,
    ar_send,
    ar_recv,
):
    rows, cols = lax.axis_size("row"), lax.axis_size("col")
    chips = rows // 2
    nx = chips // ny
    r, z = lax.axis_index("row"), lax.axis_index("col")
    core, chip = lax.rem(r, 2), r // 2
    cx, cy = chip // ny, lax.rem(chip, ny)
    share = res_ref.shape[1] // TB
    width = share // PIECES
    blocks = 2 * rows
    hb = blocks // 2
    group = 2 * ny
    rhs = res_ref.shape[0]

    def at_col(d):
        return lax.rem(z + d + cols, cols)

    def ring_dev(d):
        return (r, at_col(1 if d == 0 else -1))

    sibling = (r + 1 - 2 * core, z)

    def chip_at(dx, dy):
        return lax.rem(cx + dx, nx) * ny + lax.rem(cy + dy, ny)

    offsets = [(dx, dy) for dx in range(nx) for dy in range(ny)]
    others = sorted(
        offsets[1:], key=lambda o: (-(min(o[0], nx - o[0]) + min(o[1], ny - o[1])), o)
    )

    def remote(src, dst, ss, rs, dev):
        return pltpu.make_async_remote_copy(
            src_ref=src, dst_ref=dst, send_sem=ss, recv_sem=rs, device_id=dev, device_id_type=MESH
        )

    per_chunk = share * slots
    chunk_copies = []
    for c in range(cols):
        chunk_copies.append(
            pltpu.make_async_copy(
                tiles_hbm.at[pl.ds(c * per_chunk, per_chunk)],
                tiles.at[pl.ds(c * per_chunk, per_chunk)],
                tile_sem.at[c],
            )
        )
        chunk_copies[-1].start()

    mine = core * hb + 2 * chip
    for j in range(2):
        dirbuf[mine + j] = dir_ref[:, j * TB : (j + 1) * TB].astype(BF16)
    dirbuf[blocks] = jnp.zeros((rhs, TB), BF16)
    gbuf[blocks] = jnp.zeros((rhs, TB), BF16)
    for i in range(share):
        rowsbuf[z * share + i] = res_ref[:, i * TB : (i + 1) * TB].astype(BF16)

    barrier = pltpu.get_barrier_semaphore()
    partners = [sibling]
    partners += [(chip_at(*o) * 2 + core, z) for o in others]
    partners += [(r, at_col(d)) for d in range(1, cols)]
    for dev in partners:
        pl.semaphore_signal(barrier, inc=1, device_id=dev, device_id_type=MESH)

    shape = blocks_ref.shape
    k = blocks_ref[...]
    place = (k // 4) * 2 + k % 2 + ((k // 2) % 2) * hb
    live = lax.broadcasted_iota(jnp.int32, shape, 1) < counts_ref[...]
    block_of = jnp.where(live, place, blocks)
    keys_v[...] = jnp.zeros_like(keys_v)
    table_v[...] = jnp.zeros_like(table_v)
    keys_v[:, :slots] = block_of
    copy_keys = pltpu.make_async_copy(keys_v, keys_s, table_sem.at[0])
    copy_keys.start()
    entry = lax.broadcasted_iota(jnp.int32, shape, 0) * slots + lax.broadcasted_iota(jnp.int32, shape, 1)
    key = block_of * (shape[0] * slots) + entry
    key_rows = jnp.transpose(
        jnp.concatenate([key, jnp.zeros((shape[0], TB - slots), jnp.int32)], axis=1)
    )
    lanes = lax.broadcasted_iota(jnp.int32, (shape[0], table_v.shape[1]), 1)
    found = [jnp.zeros((1, table_v.shape[1]), jnp.int32) for _ in range(5)]
    for s in range(slots):
        below = jnp.zeros((shape[0], shape[0]), jnp.int32)
        for other in range(slots):
            below = below + jnp.where(key_rows[other : other + 1] < key[:, s : s + 1], 1, 0)
        rank = jnp.sum(below, axis=1, keepdims=True)
        block_s = block_of[:, s : s + 1]
        for i, chosen in enumerate(
            (
                jnp.where(lanes == rank, entry[:, s : s + 1], 0),
                jnp.where(lanes == rank, block_s, 0),
                jnp.where(lanes == rank + 1, block_s + 1, 0),
                jnp.where(block_s <= lanes, 1, 0),
                jnp.where(block_s == lanes, 1, 0),
            )
        ):
            found[i] = found[i] + jnp.sum(chosen, axis=0, keepdims=True)
    order, at_place, before, upto, count = found
    table_v[0:1] = order
    table_v[1:2] = jnp.where(at_place + 1 == before, 1, 0)
    table_v[2:3] = jnp.maximum(upto - 1, 0)
    table_v[3:4] = jnp.where(count > 0, 1, 0)
    copy_table = pltpu.make_async_copy(table_v, table_s, table_sem.at[1])
    copy_table.start()
    pl.semaphore_wait(barrier, len(partners))

    def sensor_tiles(sensor):
        return side_by_side([tiles[sensor * slots + s] for s in range(slots)])

    def grad_piece(buf, shard, k):
        for i in range(width):
            sensor = shard * share + k * width + i
            value = jnp.dot(buf[sensor], sensor_tiles(sensor), preferred_element_type=F32)
            for s in range(slots):
                contrib[sensor * slots + s] = value[:, s * TB : (s + 1) * TB]

    def image_piece(buf, dest, d, k):
        for i in range(width):
            sensor = dest * share + k * width + i
            picked = side_by_side([buf[jnp.clip(keys_s[sensor, s], 0, blocks)] for s in range(slots)])
            part[d, k * width + i] = dot_lanes(picked, sensor_tiles(sensor))

    def sorted_sums():
        def one(j, run):
            run = run * table_s[1, j].astype(F32) + contrib[jnp.clip(table_s[0, j], 0, contrib.shape[0] - 1)]
            prefix[j] = run
            return run

        lax.fori_loop(0, contrib.shape[0], one, jnp.zeros((rhs, TB), F32), unroll=4)

    def block_sum(k):
        return prefix[jnp.clip(table_s[2, k], 0, prefix.shape[0] - 1)] * table_s[3, k].astype(F32)

    both_ways = [(k, d) for k in range(PIECES) for d in range(2)]

    def long_way(k):
        return 0 if k < PIECES // 2 else 1

    def col_at(d, steps):
        return at_col(steps if d == 0 else -steps)

    def gather_hop(buf, n, d, t, k, landed=False):
        back = t if landed else t - 1
        ref = buf.at[pl.ds(col_at(d, -back) * share + k * width, width)]
        return remote(ref, ref, ring_send.at[n, d, t - 1, k], ring_recv.at[n, d, t - 1, k], ring_dev(d))

    def gathers(d, t, k):
        return t < HOPS or (t == HOPS and long_way(k) == d)

    def gather_step(buf, n, t):
        got = []
        for k, d in both_ways:
            if gathers(d, t, k):
                gather_hop(buf, n, d, t, k, landed=True).wait_recv()
                if gathers(d, t + 1, k):
                    gather_hop(buf, n, d, t + 1, k).start()
                got.append((col_at(d, -t), k))
        return got

    def gather_sent(buf, n):
        for t in range(1, HOPS + 1):
            for k, d in both_ways:
                if gathers(d, t, k):
                    gather_hop(buf, n, d, t, k).wait_send()

    def ring_gather(buf, n):
        for k, d in both_ways:
            gather_hop(buf, n, d, 1, k).start()
        yield
        for k in range(PIECES):
            grad_piece(buf, z, k)
        yield
        for t in range(1, HOPS + 1):
            for shard, k in gather_step(buf, n, t):
                grad_piece(buf, shard, k)
            yield
        gather_sent(buf, n)

    def image_phase(it, buf):
        n_sum, n_all = 1 + 2 * it, 2 + 2 * it
        land, whole = ringland.at[it], imgbuf.at[it]

        def sums(d, t, k):
            return 1 < t <= HOPS or (t == 1 and long_way(k) == d)

        def hop(d, t, k):
            spot = pl.ds(k * width, width)
            return remote(
                ringout.at[d, t - 1, spot],
                land.at[d, t - 1, spot],
                ring_send.at[n_sum, d, t - 1, k],
                ring_recv.at[n_sum, d, t - 1, k],
                ring_dev(d),
            )

        def partial(d, t, k):
            image_piece(buf, col_at(d, HOPS + 1 - t), d, k)

        def send(d, t, k, arrived):
            if arrived:
                hop(d, t - 1, k).wait_recv()
            for i in range(k * width, (k + 1) * width):
                value = part[d, i]
                if arrived:
                    value = value + land[d, t - 2, i].astype(F32)
                ringout[d, t - 1, i] = value.astype(BF16)
            hop(d, t, k).start()

        for k, d in both_ways:
            t = 1 if sums(d, 1, k) else 2
            partial(d, t, k)
            send(d, t, k, False)
        for k, d in both_ways:
            if sums(d, 1, k):
                partial(d, 2, k)
        yield
        for t in range(2, HOPS + 1):
            for k, d in both_ways:
                if sums(d, t - 1, k):
                    send(d, t, k, True)
            if t < HOPS:
                for k, d in both_ways:
                    partial(d, t + 1, k)
            else:
                for k in range(PIECES):
                    image_piece(buf, z, 0, k)
            yield
        for k in range(PIECES):
            for d in range(2):
                hop(d, HOPS, k).wait_recv()
            for i in range(k * width, (k + 1) * width):
                total = part[0, i]
                for d in range(2):
                    total = total + land[d, HOPS - 1, i].astype(F32)
                if it:
                    total = total + imgshare[it, i]
                imgshare[it, i] = total
                whole[z * share + i] = total.astype(BF16)
            for d in range(2):
                gather_hop(whole, n_all, d, 1, k).start()
        yield
        for k in range(PIECES):
            grad_piece(whole, z, k)
        for t in range(1, HOPS + 1):
            for shard, k in gather_step(whole, n_all, t):
                grad_piece(whole, shard, k)
            yield
        for t in range(1, HOPS + 1):
            for k, d in both_ways:
                if sums(d, t, k):
                    hop(d, t, k).wait_send()
        gather_sent(whole, n_all)

    def plane(dx):
        return lax.rem(cx + dx, nx)

    def row_gather(buf, n):
        own = buf.at[pl.ds(mine, 2)]
        for dx, dy in others:
            remote(
                own,
                own,
                agr_send.at[n],
                agr_recv.at[n, (nx - dx) % nx],
                (chip_at(dx, dy) * 2 + core, z),
            ).start()

        def forward(dx, side):
            ref = buf.at[pl.ds(side * hb + plane(dx) * group, group)]
            return remote(ref, ref, fwd_send.at[n, dx], fwd_recv.at[n, dx], sibling)

        order = sorted(range(nx), key=lambda dx: min(dx, nx - dx))
        yield
        for dx in order:
            count = group if dx else group - 2
            ref = buf.at[pl.ds(core * hb, count)]
            if count:
                remote(ref, ref, agr_send.at[n], agr_recv.at[n, dx], sibling).wait_recv()
            forward(dx, core).start()
            yield
        for dx in order:
            forward(dx, 1 - core).wait_recv()
        yield
        for dx in order:
            forward(dx, core).wait_send()
        ref = buf.at[pl.ds(0, 2 * len(others))]
        remote(ref, ref, agr_send.at[n], agr_recv.at[n, 0], sibling).wait_send()

    def row_scatter(n, out):
        def swap(dx):
            spot = pl.ds(plane(dx) * group, group)
            return remote(xout.at[spot], xland.at[n, spot], x_send.at[n, dx], x_recv.at[n, dx], sibling)

        far_first = sorted(range(nx), key=lambda dx: (-min(dx, nx - dx), dx))

        for dx in far_first:
            start = plane(dx) * group
            for b in range(group):
                xout[start + b] = block_sum((1 - core) * hb + start + b).astype(BF16)
            swap(dx).start()
        slot = {o: i for i, o in enumerate(offsets[1:])}
        for dx in far_first:
            start = plane(dx) * group
            swap(dx).wait_recv()
            for b in range(group):
                total = block_sum(core * hb + start + b) + xland[n, start + b].astype(F32)
                sbuf[start + b] = total.astype(BF16)
            for o in others:
                if o[0] == dx:
                    remote(
                        sbuf.at[pl.ds(2 * chip_at(*o), 2)],
                        rland.at[n, pl.ds(2 * slot[o], 2)],
                        rs_send.at[n],
                        rs_recv.at[n],
                        (chip_at(*o) * 2 + core, z),
                    ).start()
        for j in range(2):
            out[j] = block_sum(mine + j) + xland[n, 2 * chip + j].astype(F32)
        yield
        every = rland.at[n]
        remote(every, every, rs_send.at[n], rs_recv.at[n], sibling).wait_recv()
        for j in range(2):
            total = out[j]
            for i in range(len(others)):
                total = total + rland[n, 2 * i + j].astype(F32)
            out[j] = total
        yield
        remote(every, every, rs_send.at[n], rs_recv.at[n], sibling).wait_send()
        for dx in far_first:
            swap(dx).wait_send()

    def all_sum(n, value):
        size = value.shape[0]
        part_rows = size // 2
        whole, own_half = pl.ds(0, size), pl.ds(core * part_rows, part_rows)
        half = pl.ds(0, part_rows)
        ar_in[n, whole] = value
        first = remote(
            ar_in.at[n, whole], ar_sib.at[n, whole], ar_send.at[n, 0], ar_recv.at[n, 0], sibling
        )
        first.start()
        yield
        first.wait_recv()
        ar_x[n, chip, half] = ar_in[n, own_half] + ar_sib[n, own_half]
        mine_x = ar_x.at[n, chip, half]
        for o in others:
            remote(
                mine_x, mine_x, ar_send.at[n, 1], ar_recv.at[n, 1], (chip_at(*o) * 2 + core, z)
            ).start()
        yield
        every_x = ar_x.at[n, pl.ds(0, len(others)), half]
        remote(every_x, every_x, ar_send.at[n, 1], ar_recv.at[n, 1], sibling).wait_recv()
        total = ar_x[n, 0, half]
        for i in range(1, chips):
            total = total + ar_x[n, i, half]
        ar_z[n, z, half] = total
        mine_z = ar_z.at[n, z, half]
        for d in range(1, cols):
            remote(mine_z, mine_z, ar_send.at[n, 2], ar_recv.at[n, 2], (r, at_col(d))).start()
        yield
        every_z = ar_z.at[n, pl.ds(0, cols - 1), half]
        remote(every_z, every_z, ar_send.at[n, 2], ar_recv.at[n, 2], sibling).wait_recv()
        total = ar_z[n, 0, half]
        for i in range(1, cols):
            total = total + ar_z[n, i, half]
        ar_out[n, own_half] = total
        mine_out = ar_out.at[n, own_half]
        final = remote(mine_out, mine_out, ar_send.at[n, 3], ar_recv.at[n, 3], sibling)
        final.start()
        yield
        final.wait_recv()
        yield
        first.wait_send()
        remote(every_x, every_x, ar_send.at[n, 1], ar_recv.at[n, 1], sibling).wait_send()
        remote(every_z, every_z, ar_send.at[n, 2], ar_recv.at[n, 2], sibling).wait_send()
        final.wait_send()

    def advance(gen, times=1):
        for _ in range(times):
            next(gen, None)

    def finish(gen):
        for _ in gen:
            pass

    def wide(ref):
        return side_by_side([ref[i] for i in range(ref.shape[0])])

    def to_blocks(value):
        return [value[:, i * TB : (i + 1) * TB] for i in range(value.shape[1] // TB)]

    def pair(left, right):
        return side_by_side([left, right])

    def folded(value):
        return pair(value[: rhs // 2], value[rhs // 2 :])

    def unfolded(value):
        return jnp.concatenate([value[:, :rhs], value[:, rhs:]], axis=0)

    resid = ring_gather(rowsbuf, 0)
    advance(resid)
    direct = row_gather(dirbuf, 0)
    advance(direct)
    for c in chunk_copies:
        c.wait()
    copy_keys.wait()
    copy_table.wait()
    advance(resid, 3)
    advance(direct, nx + 1)
    image = image_phase(0, dirbuf)
    advance(image)
    finish(resid)
    advance(image)
    sorted_sums()
    rowsc = row_scatter(0, gshare)
    advance(image)
    advance(rowsc)
    advance(image)
    finish(direct)
    advance(image)

    for it in range(2):
        advance(image)
        if it == 0:
            finish(rowsc)
            curv_gamma = pair(gram(wide(imgshare.at[0])), gram(wide(gshare)))
            summed = all_sum(0, curv_gamma)
        else:
            summed = all_sum(1, folded(gram(wide(imgshare.at[1]))))
        advance(summed)
        advance(image)
        advance(summed)
        advance(image)
        advance(summed)
        advance(image)
        sorted_sums()
        rowsc = row_scatter(1 + it, hshare)
        advance(rowsc)
        finish(summed)
        finish(image)
        if it == 0:
            both = ar_out[0]
            curvature, gamma = both[:, :rhs], both[:, rhs:]
        else:
            curvature = unfolded(ar_out[1, pl.ds(0, rhs // 2)])
        inv_curv, inv_gamma = inverses([curvature, gamma])
        alpha_t = dot_high(gamma, inv_curv)
        finish(rowsc)
        step_g = to_blocks(dot_high(alpha_t, wide(hshare)))
        for j in range(2):
            gshare[j] = gshare[j] - step_g[j]
            if it == 0:
                gbuf[mine + j] = gshare[j].astype(BF16)
        if it == 0:
            direct = row_gather(gbuf, 1)
            advance(direct)
        summed = all_sum(2 + it, folded(gram(wide(gshare))))
        advance(summed)
        old_dir = dir_ref[...] if it == 0 else wide(dnext)
        old_sol = sol_ref[...] if it == 0 else sol_out[...]
        old_res = res_ref[...] if it == 0 else res_out[...]
        sol_out[...] = old_sol + dot_high(alpha_t, old_dir)
        advance(summed)
        res_out[...] = old_res - dot_high(alpha_t, wide(imgshare.at[it]))
        if it == 0:
            advance(direct, nx + 1)
            image = image_phase(1, gbuf)
            advance(image)
            advance(summed)
            advance(image)
            advance(summed)
            advance(image)
        finish(summed)
        gamma_next = unfolded(ar_out[2 + it, pl.ds(0, rhs // 2)])
        beta_t = dot_high(gamma_next, inv_gamma)
        step_d = dot_high(beta_t, old_dir)
        if it == 0:
            for i, value in enumerate(to_blocks(dot_high(beta_t, wide(imgshare.at[0])))):
                imgshare[1, i] = value
            advance(image)
            for j, value in enumerate(to_blocks(step_d)):
                dnext[j] = gshare[j] + value
            finish(direct)
            advance(image)
        else:
            dir_out[...] = wide(gshare) + step_d
        gamma = gamma_next


def hand_over(*refs):
    for source, target in zip(refs[:3], refs[3:]):
        target[...] = source[...]


def per_device(solution, residual, direction, jacobian_tiles, tile_blocks, tile_counts):
    rows, cols = lax.axis_size("row"), lax.axis_size("col")
    chips = rows // 2
    ny = 4 if chips % 4 == 0 else chips
    nx = chips // ny
    rhs = residual.shape[0]
    sensors, slots = tile_blocks.shape
    entries = sensors * slots
    blocks = 2 * rows
    share = residual.shape[1] // TB
    tile = (rhs, TB)
    vmem = pl.BlockSpec(memory_space=pltpu.VMEM)
    dma = pltpu.SemaphoreType.DMA
    results = pl.pallas_call(
        functools.partial(kernel, ny, slots),
        out_shape=[
            jax.ShapeDtypeStruct(solution.shape, F32),
            jax.ShapeDtypeStruct(residual.shape, F32),
            jax.ShapeDtypeStruct(direction.shape, F32),
        ],
        in_specs=[vmem] * 5 + [pl.BlockSpec(memory_space=pl.ANY)],
        out_specs=[vmem] * 3,
        scratch_shapes=[
            pltpu.VMEM((entries, TB, TB), BF16),
            pltpu.VMEM((entries, *tile), F32),
            pltpu.VMEM((entries, *tile), F32),
            pltpu.VMEM((blocks + 1, *tile), BF16),
            pltpu.VMEM((blocks + 1, *tile), BF16),
            pltpu.VMEM((sensors, *tile), BF16),
            pltpu.VMEM((2, sensors, *tile), BF16),
            pltpu.VMEM((2, share, *tile), F32),
            pltpu.VMEM((2, HOPS, share, *tile), BF16),
            pltpu.VMEM((2, 2, HOPS, share, *tile), BF16),
            pltpu.VMEM((2, share, *tile), F32),
            pltpu.VMEM((blocks // 2, *tile), BF16),
            pltpu.VMEM((3, blocks // 2, *tile), BF16),
            pltpu.VMEM((blocks // 2, *tile), BF16),
            pltpu.VMEM((3, 2 * (chips - 1), *tile), BF16),
            pltpu.VMEM((2, *tile), F32),
            pltpu.VMEM((2, *tile), F32),
            pltpu.VMEM((2, *tile), F32),
            pltpu.VMEM((4, rhs, TB), F32),
            pltpu.VMEM((4, rhs, TB), F32),
            pltpu.VMEM((4, chips, rhs // 2, TB), F32),
            pltpu.VMEM((4, cols, rhs // 2, TB), F32),
            pltpu.VMEM((4, rhs, TB), F32),
            pltpu.VMEM((sensors, TB), jnp.int32),
            pltpu.SMEM((sensors, TB), jnp.int32),
            pltpu.VMEM((8, -(-entries // TB) * TB), jnp.int32),
            pltpu.SMEM((8, -(-entries // TB) * TB), jnp.int32),
            dma((2,)),
            dma((cols,)),
            dma((5, 2, HOPS, PIECES)),
            dma((5, 2, HOPS, PIECES)),
            dma((2,)),
            dma((2, nx)),
            dma((2, nx)),
            dma((2, nx)),
            dma((3, nx)),
            dma((3, nx)),
            dma((3,)),
            dma((3,)),
            dma((4, 4)),
            dma((4, 4)),
        ],
        compiler_params=pltpu.CompilerParams(
            collective_id=0, has_side_effects=True, vmem_limit_bytes=58 * 1024 * 1024
        ),
    )(tile_blocks, tile_counts, solution, residual, direction, jacobian_tiles.reshape(entries, TB, TB))
    return pl.pallas_call(
        hand_over,
        out_shape=[jax.ShapeDtypeStruct(v.shape, F32) for v in results],
        in_specs=[vmem] * 3,
        out_specs=[vmem] * 3,
    )(*results)


def solution(mesh):
    both = P(None, ("row", "col"))
    return jax.shard_map(
        per_device,
        mesh=mesh,
        in_specs=(both, both, both, P("row", "col", None, None), P("row", "col"), P("row", "col")),
        out_specs=(both, both, both),
        check_vma=False,
    )
```

```python
import functools

import jax
import jax.numpy as jnp
from jax import lax
from jax.experimental import pallas as pl
from jax.experimental.pallas import tpu as pltpu
from jax.sharding import PartitionSpec as P

MESH = pl.DeviceIdType.MESH
F32, BF16 = jnp.float32, jnp.bfloat16
TB = 128
HOPS = 4
PIECES = 4
HIGH = lax.Precision.HIGHEST


def dot_high(left, right):
    return jnp.dot(left, right, precision=HIGH, preferred_element_type=F32)


def dot_lanes(left, right, precision=None):
    return lax.dot_general(
        left, right, (((1,), (1,)), ((), ())), precision=precision, preferred_element_type=F32
    )


def gram(value):
    return dot_lanes(value, value, HIGH)


def side_by_side(parts):
    return jnp.concatenate(parts, axis=1)


def inverses(matrices):
    size = matrices[0].shape[0]
    rows = lax.broadcasted_iota(jnp.int32, (size, 2 * size), 0)
    lanes = lax.broadcasted_iota(jnp.int32, (size, 2 * size), 1)
    eye = jnp.where(rows + size == lanes, 1.0, 0.0).astype(F32)[:, size:]

    def step(k, works):
        done = []
        for work in works:
            row = jnp.sum(jnp.where(rows == k, work, 0.0), axis=0, keepdims=True)
            col = jnp.sum(jnp.where(lanes == k, work, 0.0), axis=1, keepdims=True)
            pivot = jnp.sum(jnp.where(lanes[:1] == k, row, 0.0), axis=1, keepdims=True)
            row = row / pivot
            done.append(jnp.where(rows == k, row, work - col * row))
        return tuple(done)

    works = lax.fori_loop(0, size, step, tuple(side_by_side([a, eye]) for a in matrices))
    return [work[:, size:] for work in works]


def kernel(
    ny,
    slots,
    blocks_ref,
    counts_ref,
    sol_ref,
    res_ref,
    dir_ref,
    tiles_hbm,
    sol_out,
    res_out,
    dir_out,
    tiles,
    contrib,
    prefix,
    dirbuf,
    gbuf,
    rowsbuf,
    imgbuf,
    part,
    ringout,
    ringland,
    imgshare,
    xout,
    xland,
    sbuf,
    rland,
    gshare,
    hshare,
    dnext,
    ar_in,
    ar_sib,
    ar_x,
    ar_z,
    ar_out,
    keys_v,
    keys_s,
    table_v,
    table_s,
    table_sem,
    tile_sem,
    ring_send,
    ring_recv,
    agr_send,
    agr_recv,
    fwd_send,
    fwd_recv,
    x_send,
    x_recv,
    rs_send,
    rs_recv,
    ar_send,
    ar_recv,
):
    rows, cols = lax.axis_size("row"), lax.axis_size("col")
    chips = rows // 2
    nx = chips // ny
    r, z = lax.axis_index("row"), lax.axis_index("col")
    core, chip = lax.rem(r, 2), r // 2
    cx, cy = chip // ny, lax.rem(chip, ny)
    share = res_ref.shape[1] // TB
    width = share // PIECES
    blocks = 2 * rows
    hb = blocks // 2
    group = 2 * ny
    rhs = res_ref.shape[0]

    def at_col(d):
        return lax.rem(z + d + cols, cols)

    def ring_dev(d):
        return (r, at_col(1 if d == 0 else -1))

    sibling = (r + 1 - 2 * core, z)

    def chip_at(dx, dy):
        return lax.rem(cx + dx, nx) * ny + lax.rem(cy + dy, ny)

    offsets = [(dx, dy) for dx in range(nx) for dy in range(ny)]
    others = sorted(
        offsets[1:], key=lambda o: (-(min(o[0], nx - o[0]) + min(o[1], ny - o[1])), o)
    )

    def remote(src, dst, ss, rs, dev):
        return pltpu.make_async_remote_copy(
            src_ref=src, dst_ref=dst, send_sem=ss, recv_sem=rs, device_id=dev, device_id_type=MESH
        )

    per_chunk = share * slots
    chunk_copies = []
    for c in range(cols):
        chunk_copies.append(
            pltpu.make_async_copy(
                tiles_hbm.at[pl.ds(c * per_chunk, per_chunk)],
                tiles.at[pl.ds(c * per_chunk, per_chunk)],
                tile_sem.at[c],
            )
        )
        chunk_copies[-1].start()

    mine = core * hb + 2 * chip
    for j in range(2):
        dirbuf[mine + j] = dir_ref[:, j * TB : (j + 1) * TB].astype(BF16)
    dirbuf[blocks] = jnp.zeros((rhs, TB), BF16)
    gbuf[blocks] = jnp.zeros((rhs, TB), BF16)
    for i in range(share):
        rowsbuf[z * share + i] = res_ref[:, i * TB : (i + 1) * TB].astype(BF16)

    barrier = pltpu.get_barrier_semaphore()
    partners = [sibling]
    partners += [(chip_at(*o) * 2 + core, z) for o in others]
    partners += [(r, at_col(d)) for d in range(1, cols)]
    for dev in partners:
        pl.semaphore_signal(barrier, inc=1, device_id=dev, device_id_type=MESH)

    shape = (blocks_ref.shape[1], slots)
    keys_v[...] = jnp.zeros_like(keys_v)
    table_v[...] = jnp.zeros_like(table_v)
    table_v[:slots, : shape[0]] = blocks_ref[...]
    table_v[slots : slots + 1, : shape[0]] = counts_ref[...]
    by_sensor = jnp.transpose(table_v[:, :TB])[: shape[0]]
    k = by_sensor[:, :slots]
    place = (k // 4) * 2 + k % 2 + ((k // 2) % 2) * hb
    live = lax.broadcasted_iota(jnp.int32, shape, 1) < by_sensor[:, slots : slots + 1]
    block_of = jnp.where(live, place, blocks)
    keys_v[:, :slots] = block_of
    copy_keys = pltpu.make_async_copy(keys_v, keys_s, table_sem.at[0])
    copy_keys.start()
    entry = lax.broadcasted_iota(jnp.int32, shape, 0) * slots + lax.broadcasted_iota(jnp.int32, shape, 1)
    key = block_of * (shape[0] * slots) + entry
    key_rows = jnp.transpose(
        jnp.concatenate([key, jnp.zeros((shape[0], TB - slots), jnp.int32)], axis=1)
    )
    lanes = lax.broadcasted_iota(jnp.int32, (shape[0], table_v.shape[1]), 1)
    found = [jnp.zeros((1, table_v.shape[1]), jnp.int32) for _ in range(5)]
    for s in range(slots):
        below = jnp.zeros((shape[0], shape[0]), jnp.int32)
        for other in range(slots):
            below = below + jnp.where(key_rows[other : other + 1] < key[:, s : s + 1], 1, 0)
        rank = jnp.sum(below, axis=1, keepdims=True)
        block_s = block_of[:, s : s + 1]
        for i, chosen in enumerate(
            (
                jnp.where(lanes == rank, entry[:, s : s + 1], 0),
                jnp.where(lanes == rank, block_s, 0),
                jnp.where(lanes == rank + 1, block_s + 1, 0),
                jnp.where(block_s <= lanes, 1, 0),
                jnp.where(block_s == lanes, 1, 0),
            )
        ):
            found[i] = found[i] + jnp.sum(chosen, axis=0, keepdims=True)
    order, at_place, before, upto, count = found
    table_v[0:1] = order
    table_v[1:2] = jnp.where(at_place + 1 == before, 1, 0)
    table_v[2:3] = jnp.maximum(upto - 1, 0)
    table_v[3:4] = jnp.where(count > 0, 1, 0)
    copy_table = pltpu.make_async_copy(table_v, table_s, table_sem.at[1])
    copy_table.start()
    pl.semaphore_wait(barrier, len(partners))

    def sensor_tiles(sensor):
        return side_by_side([tiles[sensor * slots + s] for s in range(slots)])

    def grad_piece(buf, shard, k):
        for i in range(width):
            sensor = shard * share + k * width + i
            value = jnp.dot(buf[sensor], sensor_tiles(sensor), preferred_element_type=F32)
            for s in range(slots):
                contrib[sensor * slots + s] = value[:, s * TB : (s + 1) * TB]

    def image_piece(buf, dest, d, k):
        for i in range(width):
            sensor = dest * share + k * width + i
            picked = side_by_side([buf[jnp.clip(keys_s[sensor, s], 0, blocks)] for s in range(slots)])
            part[d, k * width + i] = dot_lanes(picked, sensor_tiles(sensor))

    def sorted_sums():
        def one(j, run):
            run = run * table_s[1, j].astype(F32) + contrib[jnp.clip(table_s[0, j], 0, contrib.shape[0] - 1)]
            prefix[j] = run
            return run

        lax.fori_loop(0, contrib.shape[0], one, jnp.zeros((rhs, TB), F32), unroll=4)

    def block_sum(k):
        return prefix[jnp.clip(table_s[2, k], 0, prefix.shape[0] - 1)] * table_s[3, k].astype(F32)

    both_ways = [(k, d) for k in range(PIECES) for d in range(2)]

    def long_way(k):
        return 0 if k < PIECES // 2 else 1

    def col_at(d, steps):
        return at_col(steps if d == 0 else -steps)

    def gather_hop(buf, n, d, t, k, landed=False):
        back = t if landed else t - 1
        ref = buf.at[pl.ds(col_at(d, -back) * share + k * width, width)]
        return remote(ref, ref, ring_send.at[n, d, t - 1, k], ring_recv.at[n, d, t - 1, k], ring_dev(d))

    def gathers(d, t, k):
        return t < HOPS or (t == HOPS and long_way(k) == d)

    def gather_step(buf, n, t):
        got = []
        for k, d in both_ways:
            if gathers(d, t, k):
                gather_hop(buf, n, d, t, k, landed=True).wait_recv()
                if gathers(d, t + 1, k):
                    gather_hop(buf, n, d, t + 1, k).start()
                got.append((col_at(d, -t), k))
        return got

    def gather_sent(buf, n):
        for t in range(1, HOPS + 1):
            for k, d in both_ways:
                if gathers(d, t, k):
                    gather_hop(buf, n, d, t, k).wait_send()

    def ring_gather(buf, n):
        for k, d in both_ways:
            gather_hop(buf, n, d, 1, k).start()
        yield
        for k in range(PIECES):
            grad_piece(buf, z, k)
        yield
        for t in range(1, HOPS + 1):
            for shard, k in gather_step(buf, n, t):
                grad_piece(buf, shard, k)
            yield
        gather_sent(buf, n)

    def image_phase(it, buf):
        n_sum, n_all = 1 + 2 * it, 2 + 2 * it
        land, whole = ringland.at[it], imgbuf.at[it]

        def sums(d, t, k):
            return 1 < t <= HOPS or (t == 1 and long_way(k) == d)

        def hop(d, t, k):
            spot = pl.ds(k * width, width)
            return remote(
                ringout.at[d, t - 1, spot],
                land.at[d, t - 1, spot],
                ring_send.at[n_sum, d, t - 1, k],
                ring_recv.at[n_sum, d, t - 1, k],
                ring_dev(d),
            )

        def partial(d, t, k):
            image_piece(buf, col_at(d, HOPS + 1 - t), d, k)

        def send(d, t, k, arrived):
            if arrived:
                hop(d, t - 1, k).wait_recv()
            for i in range(k * width, (k + 1) * width):
                value = part[d, i]
                if arrived:
                    value = value + land[d, t - 2, i].astype(F32)
                ringout[d, t - 1, i] = value.astype(BF16)
            hop(d, t, k).start()

        for k, d in both_ways:
            t = 1 if sums(d, 1, k) else 2
            partial(d, t, k)
            send(d, t, k, False)
        for k, d in both_ways:
            if sums(d, 1, k):
                partial(d, 2, k)
        yield
        for t in range(2, HOPS + 1):
            for k, d in both_ways:
                if sums(d, t - 1, k):
                    send(d, t, k, True)
            if t < HOPS:
                for k, d in both_ways:
                    partial(d, t + 1, k)
            else:
                for k in range(PIECES):
                    image_piece(buf, z, 0, k)
            yield
        for k in range(PIECES):
            for d in range(2):
                hop(d, HOPS, k).wait_recv()
            for i in range(k * width, (k + 1) * width):
                total = part[0, i]
                for d in range(2):
                    total = total + land[d, HOPS - 1, i].astype(F32)
                if it:
                    total = total + imgshare[it, i]
                imgshare[it, i] = total
                whole[z * share + i] = total.astype(BF16)
            for d in range(2):
                gather_hop(whole, n_all, d, 1, k).start()
        yield
        for k in range(PIECES):
            grad_piece(whole, z, k)
        for t in range(1, HOPS + 1):
            for shard, k in gather_step(whole, n_all, t):
                grad_piece(whole, shard, k)
            yield
        for t in range(1, HOPS + 1):
            for k, d in both_ways:
                if sums(d, t, k):
                    hop(d, t, k).wait_send()
        gather_sent(whole, n_all)

    def plane(dx):
        return lax.rem(cx + dx, nx)

    def row_gather(buf, n):
        own = buf.at[pl.ds(mine, 2)]
        for dx, dy in others:
            remote(
                own,
                own,
                agr_send.at[n],
                agr_recv.at[n, (nx - dx) % nx],
                (chip_at(dx, dy) * 2 + core, z),
            ).start()

        def forward(dx, side):
            ref = buf.at[pl.ds(side * hb + plane(dx) * group, group)]
            return remote(ref, ref, fwd_send.at[n, dx], fwd_recv.at[n, dx], sibling)

        order = sorted(range(nx), key=lambda dx: min(dx, nx - dx))
        yield
        for dx in order:
            count = group if dx else group - 2
            ref = buf.at[pl.ds(core * hb, count)]
            if count:
                remote(ref, ref, agr_send.at[n], agr_recv.at[n, dx], sibling).wait_recv()
            forward(dx, core).start()
            yield
        for dx in order:
            forward(dx, 1 - core).wait_recv()
        yield
        for dx in order:
            forward(dx, core).wait_send()
        ref = buf.at[pl.ds(0, 2 * len(others))]
        remote(ref, ref, agr_send.at[n], agr_recv.at[n, 0], sibling).wait_send()

    def row_scatter(n, out):
        def swap(dx):
            spot = pl.ds(plane(dx) * group, group)
            return remote(xout.at[spot], xland.at[n, spot], x_send.at[n, dx], x_recv.at[n, dx], sibling)

        far_first = sorted(range(nx), key=lambda dx: (-min(dx, nx - dx), dx))

        for dx in far_first:
            start = plane(dx) * group
            for b in range(group):
                xout[start + b] = block_sum((1 - core) * hb + start + b).astype(BF16)
            swap(dx).start()
        slot = {o: i for i, o in enumerate(offsets[1:])}
        for dx in far_first:
            start = plane(dx) * group
            swap(dx).wait_recv()
            for b in range(group):
                total = block_sum(core * hb + start + b) + xland[n, start + b].astype(F32)
                sbuf[start + b] = total.astype(BF16)
            for o in others:
                if o[0] == dx:
                    remote(
                        sbuf.at[pl.ds(2 * chip_at(*o), 2)],
                        rland.at[n, pl.ds(2 * slot[o], 2)],
                        rs_send.at[n],
                        rs_recv.at[n],
                        (chip_at(*o) * 2 + core, z),
                    ).start()
        for j in range(2):
            out[j] = block_sum(mine + j) + xland[n, 2 * chip + j].astype(F32)
        yield
        every = rland.at[n]
        remote(every, every, rs_send.at[n], rs_recv.at[n], sibling).wait_recv()
        for j in range(2):
            total = out[j]
            for i in range(len(others)):
                total = total + rland[n, 2 * i + j].astype(F32)
            out[j] = total
        yield
        remote(every, every, rs_send.at[n], rs_recv.at[n], sibling).wait_send()
        for dx in far_first:
            swap(dx).wait_send()

    def all_sum(n, value):
        size = value.shape[0]
        part_rows = size // 2
        whole, own_half = pl.ds(0, size), pl.ds(core * part_rows, part_rows)
        half = pl.ds(0, part_rows)
        ar_in[n, whole] = value
        first = remote(
            ar_in.at[n, whole], ar_sib.at[n, whole], ar_send.at[n, 0], ar_recv.at[n, 0], sibling
        )
        first.start()
        yield
        first.wait_recv()
        ar_x[n, chip, half] = ar_in[n, own_half] + ar_sib[n, own_half]
        mine_x = ar_x.at[n, chip, half]
        for o in others:
            remote(
                mine_x, mine_x, ar_send.at[n, 1], ar_recv.at[n, 1], (chip_at(*o) * 2 + core, z)
            ).start()
        yield
        every_x = ar_x.at[n, pl.ds(0, len(others)), half]
        remote(every_x, every_x, ar_send.at[n, 1], ar_recv.at[n, 1], sibling).wait_recv()
        total = ar_x[n, 0, half]
        for i in range(1, chips):
            total = total + ar_x[n, i, half]
        ar_z[n, z, half] = total
        mine_z = ar_z.at[n, z, half]
        for d in range(1, cols):
            remote(mine_z, mine_z, ar_send.at[n, 2], ar_recv.at[n, 2], (r, at_col(d))).start()
        yield
        every_z = ar_z.at[n, pl.ds(0, cols - 1), half]
        remote(every_z, every_z, ar_send.at[n, 2], ar_recv.at[n, 2], sibling).wait_recv()
        total = ar_z[n, 0, half]
        for i in range(1, cols):
            total = total + ar_z[n, i, half]
        ar_out[n, own_half] = total
        mine_out = ar_out.at[n, own_half]
        final = remote(mine_out, mine_out, ar_send.at[n, 3], ar_recv.at[n, 3], sibling)
        final.start()
        yield
        final.wait_recv()
        yield
        first.wait_send()
        remote(every_x, every_x, ar_send.at[n, 1], ar_recv.at[n, 1], sibling).wait_send()
        remote(every_z, every_z, ar_send.at[n, 2], ar_recv.at[n, 2], sibling).wait_send()
        final.wait_send()

    def advance(gen, times=1):
        for _ in range(times):
            next(gen, None)

    def finish(gen):
        for _ in gen:
            pass

    def wide(ref):
        return side_by_side([ref[i] for i in range(ref.shape[0])])

    def to_blocks(value):
        return [value[:, i * TB : (i + 1) * TB] for i in range(value.shape[1] // TB)]

    def pair(left, right):
        return side_by_side([left, right])

    def folded(value):
        return pair(value[: rhs // 2], value[rhs // 2 :])

    def unfolded(value):
        return jnp.concatenate([value[:, :rhs], value[:, rhs:]], axis=0)

    resid = ring_gather(rowsbuf, 0)
    advance(resid)
    direct = row_gather(dirbuf, 0)
    advance(direct)
    for c in chunk_copies:
        c.wait()
    copy_keys.wait()
    copy_table.wait()
    advance(resid, 3)
    advance(direct, nx + 1)
    image = image_phase(0, dirbuf)
    advance(image)
    finish(resid)
    advance(image)
    sorted_sums()
    rowsc = row_scatter(0, gshare)
    advance(image)
    advance(rowsc)
    advance(image)
    finish(direct)
    advance(image)

    for it in range(2):
        advance(image)
        if it == 0:
            finish(rowsc)
            curv_gamma = pair(gram(wide(imgshare.at[0])), gram(wide(gshare)))
            summed = all_sum(0, curv_gamma)
        else:
            summed = all_sum(1, folded(gram(wide(imgshare.at[1]))))
        advance(summed)
        advance(image)
        advance(summed)
        advance(image)
        advance(summed)
        advance(image)
        sorted_sums()
        rowsc = row_scatter(1 + it, hshare)
        advance(rowsc)
        finish(summed)
        finish(image)
        if it == 0:
            both = ar_out[0]
            curvature, gamma = both[:, :rhs], both[:, rhs:]
        else:
            curvature = unfolded(ar_out[1, pl.ds(0, rhs // 2)])
        inv_curv, inv_gamma = inverses([curvature, gamma])
        alpha_t = dot_high(gamma, inv_curv)
        advance(rowsc)
        step_g = to_blocks(dot_high(alpha_t, wide(hshare)))
        for j in range(2):
            gshare[j] = gshare[j] - step_g[j]
            if it == 0:
                gbuf[mine + j] = gshare[j].astype(BF16)
        if it == 0:
            direct = row_gather(gbuf, 1)
            advance(direct)
        summed = all_sum(2 + it, folded(gram(wide(gshare))))
        advance(summed)
        finish(rowsc)
        old_dir = dir_ref[...] if it == 0 else wide(dnext)
        old_sol = sol_ref[...] if it == 0 else sol_out[...]
        old_res = res_ref[...] if it == 0 else res_out[...]
        sol_out[...] = old_sol + dot_high(alpha_t, old_dir)
        advance(summed)
        res_out[...] = old_res - dot_high(alpha_t, wide(imgshare.at[it]))
        if it == 0:
            advance(direct, nx + 1)
            image = image_phase(1, gbuf)
            advance(image)
            advance(summed)
            advance(image)
            advance(summed)
            advance(image)
        advance(summed, 3)
        gamma_next = unfolded(ar_out[2 + it, pl.ds(0, rhs // 2)])
        beta_t = dot_high(gamma_next, inv_gamma)
        step_d = dot_high(beta_t, old_dir)
        if it == 0:
            for i, value in enumerate(to_blocks(dot_high(beta_t, wide(imgshare.at[0])))):
                imgshare[1, i] = value
            advance(image)
            for j, value in enumerate(to_blocks(step_d)):
                dnext[j] = gshare[j] + value
            finish(direct)
            advance(image)
        else:
            dir_out[...] = wide(gshare) + step_d
        finish(summed)
        gamma = gamma_next


def hand_over(*refs):
    for source, target in zip(refs[:3], refs[3:]):
        target[...] = source[...]


def per_device(solution, residual, direction, jacobian_tiles, tile_blocks, tile_counts):
    rows, cols = lax.axis_size("row"), lax.axis_size("col")
    chips = rows // 2
    ny = 4 if chips % 4 == 0 else chips
    nx = chips // ny
    rhs = residual.shape[0]
    sensors, slots = tile_blocks.shape
    entries = sensors * slots
    blocks = 2 * rows
    share = residual.shape[1] // TB
    tile = (rhs, TB)
    vmem = pl.BlockSpec(memory_space=pltpu.VMEM)
    dma = pltpu.SemaphoreType.DMA
    results = pl.pallas_call(
        functools.partial(kernel, ny, slots),
        out_shape=[
            jax.ShapeDtypeStruct(solution.shape, F32),
            jax.ShapeDtypeStruct(residual.shape, F32),
            jax.ShapeDtypeStruct(direction.shape, F32),
        ],
        in_specs=[vmem] * 5 + [pl.BlockSpec(memory_space=pl.ANY)],
        out_specs=[vmem] * 3,
        scratch_shapes=[
            pltpu.VMEM((entries, TB, TB), BF16),
            pltpu.VMEM((entries, *tile), F32),
            pltpu.VMEM((entries, *tile), F32),
            pltpu.VMEM((blocks + 1, *tile), BF16),
            pltpu.VMEM((blocks + 1, *tile), BF16),
            pltpu.VMEM((sensors, *tile), BF16),
            pltpu.VMEM((2, sensors, *tile), BF16),
            pltpu.VMEM((2, share, *tile), F32),
            pltpu.VMEM((2, HOPS, share, *tile), BF16),
            pltpu.VMEM((2, 2, HOPS, share, *tile), BF16),
            pltpu.VMEM((2, share, *tile), F32),
            pltpu.VMEM((blocks // 2, *tile), BF16),
            pltpu.VMEM((3, blocks // 2, *tile), BF16),
            pltpu.VMEM((blocks // 2, *tile), BF16),
            pltpu.VMEM((3, 2 * (chips - 1), *tile), BF16),
            pltpu.VMEM((2, *tile), F32),
            pltpu.VMEM((2, *tile), F32),
            pltpu.VMEM((2, *tile), F32),
            pltpu.VMEM((4, rhs, TB), F32),
            pltpu.VMEM((4, rhs, TB), F32),
            pltpu.VMEM((4, chips, rhs // 2, TB), F32),
            pltpu.VMEM((4, cols, rhs // 2, TB), F32),
            pltpu.VMEM((4, rhs, TB), F32),
            pltpu.VMEM((sensors, TB), jnp.int32),
            pltpu.SMEM((sensors, TB), jnp.int32),
            pltpu.VMEM((8, -(-entries // TB) * TB), jnp.int32),
            pltpu.SMEM((8, -(-entries // TB) * TB), jnp.int32),
            dma((2,)),
            dma((cols,)),
            dma((5, 2, HOPS, PIECES)),
            dma((5, 2, HOPS, PIECES)),
            dma((2,)),
            dma((2, nx)),
            dma((2, nx)),
            dma((2, nx)),
            dma((3, nx)),
            dma((3, nx)),
            dma((3,)),
            dma((3,)),
            dma((4, 4)),
            dma((4, 4)),
        ],
        compiler_params=pltpu.CompilerParams(
            collective_id=0, has_side_effects=True, vmem_limit_bytes=58 * 1024 * 1024
        ),
    )(tile_blocks.T, tile_counts.T, solution, residual, direction, jacobian_tiles.reshape(entries, TB, TB))
    return pl.pallas_call(
        hand_over,
        out_shape=[jax.ShapeDtypeStruct(v.shape, F32) for v in results],
        in_specs=[vmem] * 3,
        out_specs=[vmem] * 3,
    )(*results)


def solution(mesh):
    both = P(None, ("row", "col"))
    return jax.shard_map(
        per_device,
        mesh=mesh,
        in_specs=(both, both, both, P("row", "col", None, None), P("row", "col"), P("row", "col")),
        out_specs=(both, both, both),
        check_vma=False,
    )
```
